32 devices in a mesh: groups: 2 (over x), pairs: 16 (over z, y, core).
Axes of the slice: x: 2, y: 2, z: 4, core: 2. Of those that a mesh axis runs over, the one named last changes fastest.
Arguments:
- fitted_ints: bfloat16 [32, 1024, 4096], P(None, None, ('groups', 'pairs')), parts along dimension 2, may hold values from -1 to 1
- pno_basis: bfloat16 [128, 256, 64], P(('groups', 'pairs')), parts along dimension 0, may hold values from -0.375 to 0.375
- pair_occ: int32 [128, 2], P(('groups', 'pairs')), parts along dimension 0, may hold values from 0 to 31
- pair_dom: int32 [128, 256], P(('groups', 'pairs')), parts along dimension 0, may hold values from 0 to 1023, as said below
- pno_count: int32 [128], P(('groups', 'pairs')), parts along dimension 0, may hold values from 32 to 64
- pno_energy: float32 [128, 64], P(('groups', 'pairs')), parts along dimension 0, may hold values from 0.3 to 3
- occ_energy: float32 [64], P('groups'), parts along dimension 0, may hold values from -2 to -0.5
- amps: float32 [128, 64, 64], P(('groups', 'pairs')), parts along dimension 0, may hold values from -2 to 2
- cpl_pair: int32 [128, 8], P(('groups', 'pairs')), parts along dimension 0, may hold values from 0 to 63
- cpl_weight: float32 [128, 8], P(('groups', 'pairs')), parts along dimension 0, may hold values from -0.5 to 0.5
- intersections: bfloat16 [128, 8, 64, 64], P(('groups', 'pairs')), parts along dimension 0, may hold values from -1 to 1
Outputs:
- new_amps: float32 [128, 64, 64], P(('groups', 'pairs')), parts along dimension 0
- pair_ints: float32 [128, 64, 64], P(('groups', 'pairs')), parts along dimension 0
The draws below stay inside these ranges and needn't reach their ends.
There are 2 independent parts, one for each index of `groups`. The reference program is written for one: setup_inputs(seed, part) draws one part's arguments, and reference() takes and returns one part's arrays. A program takes and returns all parts, laid end to end along the dimension named above; each array names one. Nothing has to cross between parts.
Inputs may be any that keep to these rules, and one draw needn't show every extreme that they name: `pair_dom`: each row holds 256 different PAO indices.
All inputs are finite; a program needn't handle non-finite values.
Results may differ from the reference program's by a relative error of at most 0.003.
Values may be sent and summed in bfloat16 or wider, within the bound.
No kernel may reach another device: no remote copies, remote signals or barrier semaphores. Data moves between devices by JAX's collectives and lax.ppermute only.
A program may use at most 128 MiB of HBM per device.

```python
import math
import jax
import jax.numpy as jnp
from jax import lax

NOCC = 32
NPAO = 1024
DOMP = 256
NPNO = 64
NCPL = 8
NAUX = 2048
NPAIRS = 64


def draw_pair_dom(key, part):
    key = jax.random.fold_in(key, 7)
    keys = jax.random.split(key, NPAIRS)
    return jax.vmap(lambda k: jax.random.permutation(k, NPAO)[:DOMP])(keys).astype(jnp.int32)


def set_ends(result, rng, smallest, top_value):
    longest = result.shape.index(max(result.shape))
    spots = []
    for shift in (0, 1):
        where = [jax.random.randint(jax.random.fold_in(rng, axis), (), 0, length) for axis, length in enumerate(result.shape)]
        where[longest] = (where[longest] + shift) % result.shape[longest]
        spots.append(tuple(where))
    return result.at[spots[0]].set(smallest).at[spots[1]].set(top_value)


def block_scale(key, dims, cuts, low, top_value):
    loudness, own = 1.0, jax.random.fold_in(key, 6)
    for position, shards_of in cuts:
        heights = jnp.exp(jax.random.uniform(jax.random.fold_in(own, position), (shards_of,), jnp.float32, low / len(cuts), top_value / len(cuts)))
        loudness = loudness * jnp.repeat(heights, dims[position] // shards_of).reshape([-1 if axis == position else 1 for axis in range(len(dims))])
    return loudness


def gaussian(stream_key, shape, spread, limit, cuts=(), kind=jnp.bfloat16):
    drawn = jax.random.normal(stream_key, shape, jnp.float32) * spread
    if len(cuts) > 0:
        drawn = block_scale(stream_key, shape, cuts, -0.22, 0.18) * drawn
    return jnp.clip(drawn, min=-limit, max=limit).astype(kind)


def setup_inputs(seed: int = 0, part: int = 0) -> dict:
    seeds = jax.random.split(jax.random.key(seed), 12)
    part_keys = jax.random.split(jax.random.fold_in(seeds[11], part), 12)
    fitted_ints = gaussian(part_keys[0], (NOCC, NPAO, NAUX), 0.125, 1.0, ((2, 16),))
    pno_basis = gaussian(part_keys[1], (NPAIRS, DOMP, NPNO), DOMP ** -0.5, 0.375, ((0, 16),))
    pair_occ = set_ends(jax.random.randint(part_keys[2], (NPAIRS, 2), 0, NOCC), jax.random.fold_in(part_keys[2], 1), 0, NOCC - 1).astype(jnp.int32)
    pair_dom = draw_pair_dom(jax.random.fold_in(jax.random.fold_in(seeds[11], part), 71), part)
    pno_count = set_ends(jax.random.randint(part_keys[4], (NPAIRS,), NPNO // 2, NPNO + 1), jax.random.fold_in(part_keys[4], 1), NPNO // 2, NPNO).astype(jnp.int32)
    pno_energy = jnp.clip(jnp.exp(math.log(3.0) - 2.3025851 * jax.random.uniform(part_keys[5], (NPAIRS, NPNO), jnp.float32) ** block_scale(part_keys[5], (NPAIRS, NPNO), ((0, 16),), -0.2, 0.2)), 0.3, 3.0)
    occ_energy = jnp.clip(jax.random.uniform(part_keys[6], (NOCC,), jnp.float32, -2.0, -0.5), -2.0, -0.5)
    amps = gaussian(part_keys[7], (NPAIRS, NPNO, NPNO), 0.3, 2.0, ((0, 16),), jnp.float32)
    cpl_pair = set_ends(jax.random.randint(part_keys[8], (NPAIRS, NCPL), 0, NPAIRS), jax.random.fold_in(part_keys[8], 1), 0, NPAIRS - 1).astype(jnp.int32)
    cpl_weight = jnp.clip(jax.random.uniform(part_keys[9], (NPAIRS, NCPL), jnp.float32, -0.5, 0.5) * block_scale(part_keys[9], (NPAIRS, NCPL), ((0, 16),), -0.4, 0.0), -0.5, 0.5)
    intersections = gaussian(part_keys[10], (NPAIRS, NCPL, NPNO, NPNO), 0.125, 1.0, ((0, 16),))
    return dict(fitted_ints=fitted_ints, pno_basis=pno_basis, pair_occ=pair_occ, pair_dom=pair_dom, pno_count=pno_count, pno_energy=pno_energy, occ_energy=occ_energy, amps=amps, cpl_pair=cpl_pair, cpl_weight=cpl_weight, intersections=intersections)


def reference(fitted_ints, pno_basis, pair_occ, pair_dom, pno_count, pno_energy, occ_energy, amps, cpl_pair, cpl_weight, intersections):
    def one_pair(items):
        occ, dom, basis = items
        rows_i = jnp.take(fitted_ints[occ[0]], dom, axis=0)
        rows_j = jnp.take(fitted_ints[occ[1]], dom, axis=0)
        fit_i = jnp.dot(rows_i.T, basis, preferred_element_type=jnp.float32).astype(jnp.bfloat16)
        fit_j = jnp.dot(rows_j.T, basis, preferred_element_type=jnp.float32).astype(jnp.bfloat16)
        return jnp.dot(fit_i.T, fit_j, preferred_element_type=jnp.float32)

    exch = lax.map(one_pair, (pair_occ, pair_dom, pno_basis))
    chosen = amps[cpl_pair] * cpl_weight[:, :, None, None]
    sfull = intersections.astype(jnp.float32)
    half = jnp.einsum("pcae,pcef->pcaf", sfull, chosen, precision=lax.Precision.HIGHEST)
    coupled = jnp.einsum("pcaf,pcbf->pab", half, sfull, precision=lax.Precision.HIGHEST)
    occ_pair = occ_energy[pair_occ[:, 0]] + occ_energy[pair_occ[:, 1]]
    denom = pno_energy[:, :, None] + pno_energy[:, None, :] - occ_pair[:, None, None]
    resid = exch + denom * amps + coupled
    index = jnp.arange(amps.shape[1], dtype=jnp.int32)
    live = (index[None, :] < pno_count[:, None]).astype(jnp.float32)
    mask = live[:, :, None] * live[:, None, :]
    new_amps = mask * (amps - resid / (denom + 0.5))
    return new_amps, mask * exch
```

```python
import functools

import jax
import jax.numpy as jnp
from jax import lax
from jax.experimental import pallas as pl
from jax.experimental.pallas import tpu as pltpu
from jax.sharding import PartitionSpec as P

NT = (((1,), (1,)), ((), ()))
VMEM = pl.BlockSpec(memory_space=pltpu.VMEM)
SMEM = pl.BlockSpec(memory_space=pltpu.SMEM)
LIMIT = 24 * 1024 * 1024
ROWS = 16
GROUP = 8


def code(index):
    low = 128 + jnp.bitwise_and(index, 127)
    return lax.shift_left(low, lax.shift_right_logical(index, 7)).astype(jnp.float32).astype(jnp.bfloat16)


def pack_kernel(basis_ref, dom_ref, occ_ref, amps_ref, out_ref):
    per, dom, npno = basis_ref.shape
    for p in range(per):
        out_ref[p * npno : (p + 1) * npno, :] = basis_ref[p].T
    base = per * npno
    out_ref[base : base + npno, :] = jnp.concatenate(
        [amps_ref[p].astype(jnp.bfloat16) for p in range(per)], axis=1
    )
    lane = lax.broadcasted_iota(jnp.int32, (1, dom), 1)
    orbitals = jnp.zeros((1, dom), jnp.int32)
    for p in range(per):
        for t in range(2):
            orbitals = jnp.where(lane == 2 * p + t, occ_ref[p, t], orbitals)
    tail = jnp.concatenate(
        [
            code(dom_ref[...]).astype(jnp.float32),
            orbitals.astype(jnp.float32),
            jnp.zeros((ROWS - per - 1, dom), jnp.float32),
        ],
        axis=0,
    )
    out_ref[base + npno :, :] = tail.astype(jnp.bfloat16)


def exch_kernel(count, per, npno, *refs):
    blocks, fitted_ref, out_ref = refs[:count], refs[count], refs[count + 1]
    held_ref, occ_ref, b_ref, f_ref, sem = refs[count + 2 :]
    npao, width = fitted_ref.shape[1:]
    dom = blocks[0].shape[1]
    base = (per + 1) * npno
    for k in range(count):
        tail = blocks[k][base : base + ROWS, :].astype(jnp.float32)
        held_ref[k : k + 1, :] = tail[per : per + 1, :128].astype(jnp.int32)
    copy = pltpu.make_async_copy(held_ref, occ_ref, sem)
    copy.start()
    codes = code(lax.broadcasted_iota(jnp.int32, (1, npao), 1))
    zero, one = jnp.bfloat16(0), jnp.bfloat16(1)

    def expand(slot, pair):
        k, p = divmod(pair, per)
        row = blocks[k][base + p : base + p + 1, :]
        column = jnp.broadcast_to(row, (128, dom)).T
        hits = jnp.concatenate(
            [jnp.where(column == codes[:, q : q + 128], one, zero) for q in range(0, npao, 128)], axis=1
        )
        b_ref[slot] = jnp.dot(
            blocks[k][p * npno : (p + 1) * npno, :], hits, preferred_element_type=jnp.float32
        ).astype(jnp.bfloat16)

    def fit(slot, pair):
        k, p = divmod(pair, per)
        slabs = jnp.concatenate([fitted_ref[occ_ref[k, 2 * p + t]] for t in range(2)], axis=1)
        f_ref[slot] = jnp.dot(b_ref[slot], slabs, preferred_element_type=jnp.float32).astype(jnp.bfloat16)

    def contract(slot, pair):
        k, p = divmod(pair, per)
        both = f_ref[slot]
        out_ref[k, :, p * npno : (p + 1) * npno] = lax.dot_general(
            both[:, :width], both[:, width:], NT, preferred_element_type=jnp.float32
        )

    pairs = count * per
    for first in range(0, pairs, GROUP):
        group = list(enumerate(range(first, min(first + GROUP, pairs))))
        for slot, pair in group:
            expand(slot, pair)
        if first == 0:
            copy.wait()
        for slot, pair in group:
            fit(slot, pair)
        for slot, pair in group:
            contract(slot, pair)


def coupled_kernel(count, *refs):
    blocks = refs[:count]
    where_ref, weight_ref, inter_ref, occ_ref, count_ref, occ_energy_ref, energy_ref, amps_ref = refs[count : count + 8]
    kept_ref, factor_ref, live_ref, all_ref, half_ref = refs[count + 8 :]
    per, ncpl, npno = inter_ref.shape[:3]
    base = per * npno
    for k in range(count):
        rows = blocks[k][base : base + npno, :]
        for p in range(per):
            all_ref[k * per + p] = rows[:, p * npno : (p + 1) * npno]
    for p in range(per):
        for c in range(ncpl):
            half_ref[p * ncpl + c] = weight_ref[p, c] * jnp.dot(
                inter_ref[p, c], all_ref[where_ref[p, c]], preferred_element_type=jnp.float32
            )
    row = lax.broadcasted_iota(jnp.int32, (npno, npno), 0)
    col = lax.broadcasted_iota(jnp.int32, (npno, npno), 1)
    for p in range(per):
        total = jnp.zeros((npno, npno), jnp.float32)
        for c in range(ncpl):
            half = half_ref[p * ncpl + c]
            high = half.astype(jnp.bfloat16)
            low = (half - high.astype(jnp.float32)).astype(jnp.bfloat16)
            inter = inter_ref[p, c]
            total = total + lax.dot_general(high, inter, NT, preferred_element_type=jnp.float32)
            total = total + lax.dot_general(low, inter, NT, preferred_element_type=jnp.float32)
        here = slice(p * npno, (p + 1) * npno)
        across = jnp.broadcast_to(energy_ref[p : p + 1, :], (npno, npno))
        occ_pair = occ_energy_ref[occ_ref[p, 0]] + occ_energy_ref[occ_ref[p, 1]]
        denom = across.T + across - occ_pair
        live = jnp.where((row < count_ref[p]) & (col < count_ref[p]), jnp.float32(1), jnp.float32(0))
        factor = live / (denom + 0.5)
        amps = amps_ref[p]
        kept_ref[:, here] = live * amps - factor * (denom * amps + total)
        factor_ref[:, here] = factor
        live_ref[:, here] = live


def finish_kernel(own_ref, came_ref, kept_ref, factor_ref, live_ref, new_ref, ints_ref):
    per, npno = new_ref.shape[:2]
    exch = own_ref[...] + came_ref[...]
    new = kept_ref[...] - exch * factor_ref[...]
    ints = exch * live_ref[...]
    for p in range(per):
        new_ref[p] = new[:, p * npno : (p + 1) * npno]
        ints_ref[p] = ints[:, p * npno : (p + 1) * npno]


def shards(
    fitted_ints,
    pno_basis,
    pair_occ,
    pair_dom,
    pno_count,
    pno_energy,
    occ_energy,
    amps,
    cpl_pair,
    cpl_weight,
    intersections,
):
    ndev = lax.axis_size("pairs")
    per, dom, npno = pno_basis.shape
    ncpl = cpl_pair.shape[1]
    npao, width = fitted_ints.shape[1:]
    params = pltpu.CompilerParams(vmem_limit_bytes=LIMIT)
    me = lax.axis_index("pairs")
    steps = [1 << b for b in reversed(range(1, ndev.bit_length() - 1))]

    def swap(array, mask):
        return lax.ppermute(array, "pairs", [(d, d ^ mask) for d in range(ndev)])

    block = pl.pallas_call(
        pack_kernel,
        out_shape=jax.ShapeDtypeStruct(((per + 1) * npno + ROWS, dom), jnp.bfloat16),
        in_specs=[VMEM, VMEM, SMEM, VMEM],
        out_specs=VMEM,
        compiler_params=params,
    )(pno_basis, pair_dom, pair_occ, amps)

    blocks = {0: block}
    for mask in steps:
        for m in sorted(blocks):
            blocks[m ^ mask] = swap(blocks[m], mask)
    for m in sorted(blocks):
        blocks[m ^ 1] = swap(blocks[m], 1)

    def exchange(which):
        count = len(which)
        out = pl.pallas_call(
            functools.partial(exch_kernel, count, per, npno),
            out_shape=jax.ShapeDtypeStruct((count, npno, per * npno), jnp.float32),
            in_specs=[VMEM] * (count + 1),
            out_specs=VMEM,
            scratch_shapes=[
                pltpu.VMEM((8, 128), jnp.int32),
                pltpu.SMEM((8, 128), jnp.int32),
                pltpu.VMEM((GROUP, npno, npao), jnp.bfloat16),
                pltpu.VMEM((GROUP, npno, 2 * width), jnp.bfloat16),
                pltpu.SemaphoreType.DMA,
            ],
            compiler_params=params,
            cost_estimate=pl.CostEstimate(
                flops=2 * count * per * npno * npao * (dom + 2 * width),
                bytes_accessed=8 << 20,
                transcendentals=0,
            ),
        )(*[blocks[m] for m in which], fitted_ints)
        return out

    even = [0]
    for mask in steps:
        even += [m ^ mask for m in even]
    total = {}
    for first in range(0, len(even), 2):
        mine = even[first : first + 2]
        part = exchange(mine + [m ^ 1 for m in mine])
        n = len(mine)
        came = swap(part[n:], 1)
        for k, m in enumerate(mine):
            total[m] = part[k] + came[k]

    where = jnp.bitwise_xor(cpl_pair // per, me) * per + cpl_pair % per
    kept, factor, live = pl.pallas_call(
        functools.partial(coupled_kernel, ndev),
        out_shape=[jax.ShapeDtypeStruct((npno, per * npno), jnp.float32)] * 3,
        in_specs=[VMEM] * ndev + [SMEM, SMEM, VMEM, SMEM, SMEM, SMEM, VMEM, VMEM],
        out_specs=[VMEM] * 3,
        scratch_shapes=[
            pltpu.VMEM((ndev * per, npno, npno), jnp.bfloat16),
            pltpu.VMEM((per * ncpl, npno, npno), jnp.float32),
        ],
        compiler_params=params,
    )(
        *[blocks[m] for m in range(ndev)],
        where,
        cpl_weight,
        intersections,
        pair_occ,
        pno_count,
        occ_energy,
        pno_energy,
        amps,
    )

    came = None
    for mask in reversed(steps):
        send = [m for m in even if m & mask and m in total]
        got = swap(tuple(total[m] for m in send), mask)
        for m, array in zip(send, got):
            if m ^ mask == 0 and mask == steps[0]:
                came = array
            else:
                total[m ^ mask] = total[m ^ mask] + array
            del total[m]

    return pl.pallas_call(
        finish_kernel,
        out_shape=[jax.ShapeDtypeStruct((per, npno, npno), jnp.float32)] * 2,
        in_specs=[VMEM] * 5,
        out_specs=[VMEM] * 2,
        compiler_params=params,
    )(total[0], came, kept, factor, live)


def solution(mesh):
    both = ("groups", "pairs")
    in_specs = (
        P(None, None, both),
        P(both, None, None),
        P(both, None),
        P(both, None),
        P(both),
        P(both, None),
        P("groups"),
        P(both, None, None),
        P(both, None),
        P(both, None),
        P(both, None, None, None),
    )
    out_specs = (P(both, None, None), P(both, None, None))

    def run(*args):
        return tuple(jax.shard_map(shards, mesh=mesh, in_specs=in_specs, out_specs=out_specs, check_vma=False)(*args))

    return run
```

```python
import functools

import jax
import jax.numpy as jnp
from jax import lax
from jax.experimental import pallas as pl
from jax.experimental.pallas import tpu as pltpu
from jax.sharding import PartitionSpec as P

NT = (((1,), (1,)), ((), ()))
VMEM = pl.BlockSpec(memory_space=pltpu.VMEM)
HBM = pl.BlockSpec(memory_space=pltpu.HBM)
SMEM = pl.BlockSpec(memory_space=pltpu.SMEM)
SENT = jnp.bfloat16
LIMIT = 16 << 20
ROWS = 16
CALL = 2
COST = 300_000_000
GROUP = 16


def code(index):
    low = 128 + jnp.bitwise_and(index, 127)
    return lax.shift_left(low, lax.shift_right_logical(index, 7)).astype(jnp.float32).astype(jnp.bfloat16)


def pack_kernel(basis_ref, dom_ref, occ_ref, amps_ref, out_ref, again_ref, dom_in, occ_in, amps_in, sems):
    per, npno, dom = basis_ref.shape
    base = per * npno
    copies = [
        pltpu.make_async_copy(amps_ref, amps_in, sems.at[0]),
        pltpu.make_async_copy(dom_ref, dom_in, sems.at[1]),
        pltpu.make_async_copy(occ_ref, occ_in, sems.at[2]),
    ]
    for p in range(per):
        for k, ref in enumerate((out_ref, again_ref)):
            rows = ref.at[pl.ds(p * npno, npno)]
            copies.append(pltpu.make_async_copy(basis_ref.at[p], rows, sems.at[3 + 2 * p + k]))
    for copy in copies:
        copy.start()
    for copy in copies:
        copy.wait()
    lane = lax.broadcasted_iota(jnp.int32, (1, dom), 1)
    orbitals = jnp.zeros((1, dom), jnp.int32)
    for p in range(per):
        for t in range(2):
            orbitals = jnp.where(lane == 2 * p + t, occ_in[t, p], orbitals)
    tail = jnp.concatenate(
        [
            code(dom_in[...]).astype(jnp.float32),
            orbitals.astype(jnp.float32),
            jnp.zeros((ROWS - per - 1, dom), jnp.float32),
        ],
        axis=0,
    )
    for ref in (out_ref, again_ref):
        ref[base : base + npno, :] = jnp.concatenate(
            [amps_in[p].astype(jnp.bfloat16) for p in range(per)], axis=1
        )
        ref[base + npno :, :] = tail.astype(jnp.bfloat16)


def read_orbitals(blocks, per, npno, held_ref, occ_ref, sem):
    base = (per + 1) * npno
    for k, block in enumerate(blocks):
        tail = block[base : base + ROWS, :].astype(jnp.float32)
        held_ref[k : k + 1, :] = tail[per : per + 1, :128].astype(jnp.int32)
    return pltpu.make_async_copy(held_ref, occ_ref, sem)


def contract(both, width):
    return lax.dot_general(both[:, :width], both[:, width:], NT, preferred_element_type=jnp.float32)


def expand(block, p, codes, out_ref, at):
    npno, dom = out_ref.shape[1], block.shape[1]
    base = block.shape[0] - ROWS + p
    column = jnp.broadcast_to(block[base : base + 1, :], (128, dom)).T
    zero, one = jnp.bfloat16(0), jnp.bfloat16(1)
    hits = jnp.concatenate(
        [jnp.where(column == codes[:, q : q + 128], one, zero) for q in range(0, codes.shape[1], 128)], axis=1
    )
    out_ref[at] = jnp.dot(
        block[p * npno : (p + 1) * npno, :], hits, preferred_element_type=jnp.float32
    ).astype(jnp.bfloat16)


def fit(wide, fitted_ref, orbitals, f_ref, at):
    slabs = jnp.concatenate([fitted_ref[o] for o in orbitals], axis=1)
    f_ref[at] = jnp.dot(wide, slabs, preferred_element_type=jnp.float32).astype(jnp.bfloat16)


def batches(count):
    return [range(first, min(first + GROUP, count)) for first in range(0, count, GROUP)]


def exch_kernel(count, per, npno, *refs):
    blocks, fitted_ref = refs[:count], refs[count]
    outs, (held_ref, occ_ref, wide_ref, f_ref, sem) = refs[-7:-5], refs[-5:]
    npao, width = fitted_ref.shape[1:]
    orbitals = read_orbitals(blocks, per, npno, held_ref, occ_ref, sem)
    orbitals.start()
    codes = code(lax.broadcasted_iota(jnp.int32, (1, npao), 1))
    for group in batches(count * per):
        for at, pair in enumerate(group):
            k, p = divmod(pair, per)
            expand(blocks[k], p, codes, wide_ref, at)
        if group[0] == 0:
            orbitals.wait()
        for at, pair in enumerate(group):
            k, p = divmod(pair, per)
            fit(wide_ref[at], fitted_ref, [occ_ref[k, 2 * p + t] for t in range(2)], f_ref, at)
        for at, pair in enumerate(group):
            k, p = divmod(pair, per)
            half, k = divmod(k, count // 2)
            outs[half][k, :, p * npno : (p + 1) * npno] = contract(f_ref[at], width)


def gate_kernel(*refs):
    pass


def sum_kernel(plan, *refs):
    outs = refs[len(refs) - len(plan) :]
    for out_ref, terms in zip(outs, plan):
        for k, (first, *others) in enumerate(terms):
            total = refs[first[0]][first[1]].astype(jnp.float32)
            for ref, at in others:
                total = total + refs[ref][at].astype(jnp.float32)
            out_ref[k] = total.astype(out_ref.dtype)


def coupled_kernel(count, *refs):
    blocks, refs = refs[:count], refs[count:]
    where_ref, weight_ref, inter_ref, occ_ref, count_ref, occ_energy_ref, energy_ref, amps_ref = refs[:8]
    kept_ref, factor_ref, live_ref, all_ref, half_ref = refs[8:]
    per, ncpl, npno = inter_ref.shape[:3]
    for k in range(count):
        rows = blocks[k][per * npno : (per + 1) * npno, :]
        for p in range(per):
            all_ref[k * per + p] = rows[:, p * npno : (p + 1) * npno]
    for p in range(per):
        for c in range(ncpl):
            half_ref[p * ncpl + c] = weight_ref[p, c] * jnp.dot(
                inter_ref[p, c], all_ref[where_ref[p, c]], preferred_element_type=jnp.float32
            )
    row = lax.broadcasted_iota(jnp.int32, (npno, npno), 0)
    col = lax.broadcasted_iota(jnp.int32, (npno, npno), 1)
    for p in range(per):
        total = jnp.zeros((npno, npno), jnp.float32)
        for c in range(ncpl):
            half = half_ref[p * ncpl + c]
            high = half.astype(jnp.bfloat16)
            low = (half - high.astype(jnp.float32)).astype(jnp.bfloat16)
            inter = inter_ref[p, c]
            total = total + lax.dot_general(high, inter, NT, preferred_element_type=jnp.float32)
            total = total + lax.dot_general(low, inter, NT, preferred_element_type=jnp.float32)
        here = slice(p * npno, (p + 1) * npno)
        across = jnp.broadcast_to(energy_ref[p : p + 1, :], (npno, npno))
        occ_pair = occ_energy_ref[occ_ref[0, p]] + occ_energy_ref[occ_ref[1, p]]
        denom = across.T + across - occ_pair
        live = jnp.where((row < count_ref[p]) & (col < count_ref[p]), jnp.float32(1), jnp.float32(0))
        factor = live / (denom + 0.5)
        amps = amps_ref[p]
        kept_ref[:, here] = live * amps - factor * (denom * amps + total)
        factor_ref[:, here] = factor
        live_ref[:, here] = live


def finish_kernel(own_ref, came_ref, kept_ref, factor_ref, live_ref, new_ref, ints_ref):
    per, npno = new_ref.shape[:2]
    exch = own_ref[0] + came_ref[0].astype(jnp.float32)
    new = kept_ref[...] - exch * factor_ref[...]
    ints = exch * live_ref[...]
    for p in range(per):
        new_ref[p] = new[:, p * npno : (p + 1) * npno]
        ints_ref[p] = ints[:, p * npno : (p + 1) * npno]


def shards(
    fitted_ints,
    pno_basis,
    pair_occ,
    pair_dom,
    pno_count,
    pno_energy,
    occ_energy,
    amps,
    cpl_pair,
    cpl_weight,
    intersections,
):
    ndev = lax.axis_size("pairs")
    per, dom, npno = pno_basis.shape
    ncpl = cpl_pair.shape[1]
    npao, width = fitted_ints.shape[1:]
    params = pltpu.CompilerParams(vmem_limit_bytes=LIMIT)
    me = lax.axis_index("pairs")
    steps = [1 << b for b in reversed(range(1, ndev.bit_length() - 1))]

    def swap(array, mask):
        return lax.ppermute(array, "pairs", [(d, d ^ mask) for d in range(ndev)])

    first_block, block = pl.pallas_call(
        pack_kernel,
        out_shape=[jax.ShapeDtypeStruct(((per + 1) * npno + ROWS, dom), jnp.bfloat16)] * 2,
        in_specs=[HBM] * 4,
        out_specs=[VMEM] * 2,
        scratch_shapes=[
            pltpu.VMEM((per, dom), jnp.int32),
            pltpu.SMEM((2, per), jnp.int32),
            pltpu.VMEM((per, npno, npno), jnp.float32),
            pltpu.SemaphoreType.DMA((3 + 2 * per,)),
        ],
        compiler_params=pltpu.CompilerParams(vmem_limit_bytes=62 << 20),
    )(jnp.swapaxes(pno_basis, 1, 2), pair_dom, pair_occ.T, amps)

    def estimate(flops):
        return pl.CostEstimate(flops=flops, bytes_accessed=1 << 20, transcendentals=0)

    def gate(array, after=(), flops=0, held=False):
        return pl.pallas_call(
            gate_kernel,
            out_shape=jax.ShapeDtypeStruct(array.shape, array.dtype),
            in_specs=[HBM] * (1 + len(after)) + [VMEM] * held,
            out_specs=HBM,
            input_output_aliases={0: 0},
            compiler_params=params,
            cost_estimate=estimate(flops),
        )(array, *after, *[fitted_ints] * held)

    mine, came, chain, back = {}, {}, [], []

    def exchange(which, cost=COST):
        count = 2 * len(which)
        after = chain[-1:] + back[:-1][-1:]
        out = pl.pallas_call(
            functools.partial(exch_kernel, count, per, npno),
            out_shape=[jax.ShapeDtypeStruct((len(which), npno, per * npno), jnp.float32)] * 2,
            in_specs=[VMEM] * (count + 1) + [HBM] * len(after),
            out_specs=[VMEM] * 2,
            scratch_shapes=[
                pltpu.VMEM((8, 128), jnp.int32),
                pltpu.SMEM((8, 128), jnp.int32),
                pltpu.VMEM((GROUP, npno, npao), jnp.bfloat16),
                pltpu.VMEM((GROUP, npno, 2 * width), jnp.bfloat16),
                pltpu.SemaphoreType.DMA,
            ],
            compiler_params=params,
            cost_estimate=estimate(cost * count * per),
        )(*[blocks[m] for m in which], *[blocks[m ^ 1] for m in which], fitted_ints, *after)
        chain.append(out[0])
        got = swap(out[1], 1)
        back.append(got)
        for k, m in enumerate(which):
            mine[m], came[m] = (out[0], k), (got, k)

    def add_up(plan, dtypes, after=()):
        arrays = []
        for terms in plan:
            for term in terms:
                for array, _ in term:
                    if not any(array is a for a in arrays):
                        arrays.append(array)
        number = lambda array: [array is a for a in arrays].index(True)
        return pl.pallas_call(
            functools.partial(
                sum_kernel, [[[(number(array), at) for array, at in term] for term in terms] for terms in plan]
            ),
            out_shape=[
                jax.ShapeDtypeStruct((len(terms), npno, per * npno), dtype) for terms, dtype in zip(plan, dtypes)
            ],
            in_specs=[VMEM] * len(arrays) + [HBM] * len(after),
            out_specs=[VMEM] * len(plan),
            compiler_params=params,
        )(*arrays, *after)

    top, rest, last = steps[0], steps[1:], steps[-1]
    blocks = {top: swap(first_block, top)}
    block = blocks[0] = gate(block, (), 32 * COST)
    for mask in rest + [1]:
        blocks[mask] = swap(block, mask)
    exchange([0])
    for m in rest:
        blocks[m ^ 1] = swap(blocks[m], 1)
    exchange(rest[::-1])
    for m in rest[:-1]:
        blocks[m ^ last] = swap(blocks[m], last)
        blocks[m ^ last ^ 1] = swap(blocks[m ^ last], 1)
    blocks[top] = gate(blocks[top], chain[-1:], held=True)
    for mask in (rest[0], last):
        blocks[top ^ mask] = swap(blocks[top], mask)
    blocks[top ^ 1] = swap(blocks[top], 1)
    exchange([rest[0] ^ last, top])
    blocks[top ^ rest[0]] = gate(blocks[top ^ rest[0]], chain[-1:], held=True)
    even = [0, top]
    for mask in rest:
        for m in list(even):
            if m ^ mask not in blocks:
                blocks[m ^ mask] = swap(blocks[m], mask)
            even.append(m ^ mask)
    own = [0]
    for mask in steps[:-1]:
        own += [m ^ mask for m in own]
    far = [m ^ last for m in own]
    left = [m for m in far[:-1] + own if m not in mine]
    for m in left:
        if m ^ 1 not in blocks:
            blocks[m ^ 1] = swap(blocks[m], 1)
    for first in range(0, len(left), CALL):
        exchange(left[first : first + CALL])
    blocks[far[-1]] = gate(blocks[far[-1]], chain[-1:], 32 * COST)
    blocks[far[-1] ^ 1] = swap(blocks[far[-1]], 1)
    exchange(far[-1:])

    ready = add_up([[[mine[m], came[m]] for m in far[:-1]]], [SENT])[0]
    final = add_up([[[mine[m], came[m]] for m in far[-1:]]], [SENT])[0]
    terms = [[mine[m], came[m]] for m in own]
    ready, final = swap(ready, last), swap(final, last)
    for k, term in enumerate(terms):
        term.append((ready, k) if k < len(own) - 1 else (final, 0))

    away = jnp.bitwise_xor(cpl_pair // per, me)
    where = away * per + cpl_pair % per
    kept, factor, live = pl.pallas_call(
        functools.partial(coupled_kernel, ndev),
        out_shape=[jax.ShapeDtypeStruct((npno, per * npno), jnp.float32)] * 3,
        in_specs=[VMEM] * ndev + [SMEM, SMEM, VMEM, SMEM, SMEM, SMEM, VMEM, VMEM],
        out_specs=[VMEM] * 3,
        scratch_shapes=[
            pltpu.VMEM((ndev * per, npno, npno), jnp.bfloat16),
            pltpu.VMEM((per * ncpl, npno, npno), jnp.float32),
        ],
        compiler_params=params,
        cost_estimate=estimate(8 * COST),
    )(
        *[blocks[m] for m in range(ndev)],
        where,
        cpl_weight,
        intersections,
        pair_occ.T,
        pno_count,
        occ_energy,
        pno_energy,
        amps,
    )

    for mask in reversed(steps[:-1]):
        half = len(terms) // 2
        keep, send = add_up([terms[:half], terms[half:]], [jnp.float32, SENT], [kept] if mask == steps[-2] else [])
        send = swap(send, mask)
        terms = [[(keep, k), (send, k)] for k in range(half)]

    return pl.pallas_call(
        finish_kernel,
        out_shape=[jax.ShapeDtypeStruct((per, npno, npno), jnp.float32)] * 2,
        in_specs=[VMEM] * 5,
        out_specs=[VMEM] * 2,
        compiler_params=params,
    )(keep, send, kept, factor, live)


def solution(mesh):
    both = ("groups", "pairs")
    in_specs = (
        P(None, None, both),
        P(both, None, None),
        P(both, None),
        P(both, None),
        P(both),
        P(both, None),
        P("groups"),
        P(both, None, None),
        P(both, None),
        P(both, None),
        P(both, None, None, None),
    )
    out_specs = (P(both, None, None), P(both, None, None))

    def run(*args):
        return tuple(jax.shard_map(shards, mesh=mesh, in_specs=in_specs, out_specs=out_specs, check_vma=False)(*args))

    return run
```

```python
import functools

import jax
import jax.numpy as jnp
from jax import lax
from jax.experimental import pallas as pl
from jax.experimental.pallas import tpu as pltpu
from jax.sharding import PartitionSpec as P

NT = (((1,), (1,)), ((), ()))
VMEM = pl.BlockSpec(memory_space=pltpu.VMEM)
HBM = pl.BlockSpec(memory_space=pltpu.HBM)
SMEM = pl.BlockSpec(memory_space=pltpu.SMEM)
SENT = jnp.bfloat16
LIMIT = 16 << 20
ROWS = 16
CALL = 2
COST = 300_000_000
GROUP = 16


def code(index):
    low = 128 + jnp.bitwise_and(index, 127)
    return lax.shift_left(low, lax.shift_right_logical(index, 7)).astype(jnp.float32).astype(jnp.bfloat16)


def pack_kernel(basis_ref, dom_ref, occ_ref, amps_ref, out_ref, again_ref, dom_in, occ_in, amps_in, sems):
    per, npno, dom = basis_ref.shape
    base = per * npno
    copies = [
        pltpu.make_async_copy(amps_ref, amps_in, sems.at[0]),
        pltpu.make_async_copy(dom_ref, dom_in, sems.at[1]),
        pltpu.make_async_copy(occ_ref, occ_in, sems.at[2]),
    ]
    for p in range(per):
        for k, ref in enumerate((out_ref, again_ref)):
            rows = ref.at[pl.ds(p * npno, npno)]
            copies.append(pltpu.make_async_copy(basis_ref.at[p], rows, sems.at[3 + 2 * p + k]))
    for copy in copies:
        copy.start()
    for copy in copies:
        copy.wait()
    lane = lax.broadcasted_iota(jnp.int32, (1, dom), 1)
    orbitals = jnp.zeros((1, dom), jnp.int32)
    for p in range(per):
        for t in range(2):
            orbitals = jnp.where(lane == 2 * p + t, occ_in[t, p], orbitals)
    tail = jnp.concatenate(
        [
            code(dom_in[...]).astype(jnp.float32),
            orbitals.astype(jnp.float32),
            jnp.zeros((ROWS - per - 1, dom), jnp.float32),
        ],
        axis=0,
    )
    for ref in (out_ref, again_ref):
        ref[base : base + npno, :] = jnp.concatenate(
            [amps_in[p].astype(jnp.bfloat16) for p in range(per)], axis=1
        )
        ref[base + npno :, :] = tail.astype(jnp.bfloat16)


def read_orbitals(blocks, per, npno, held_ref, occ_ref, sem):
    base = (per + 1) * npno
    for k, block in enumerate(blocks):
        tail = block[base : base + ROWS, :].astype(jnp.float32)
        held_ref[k : k + 1, :] = tail[per : per + 1, :128].astype(jnp.int32)
    return pltpu.make_async_copy(held_ref, occ_ref, sem)


def contract(both, width):
    return lax.dot_general(both[:, :width], both[:, width:], NT, preferred_element_type=jnp.float32)


def expand(block, p, codes, out_ref, at):
    npno, dom = out_ref.shape[1], block.shape[1]
    base = block.shape[0] - ROWS + p
    column = jnp.broadcast_to(block[base : base + 1, :], (128, dom)).T
    zero, one = jnp.bfloat16(0), jnp.bfloat16(1)
    hits = jnp.concatenate(
        [jnp.where(column == codes[:, q : q + 128], one, zero) for q in range(0, codes.shape[1], 128)], axis=1
    )
    out_ref[at] = jnp.dot(
        block[p * npno : (p + 1) * npno, :], hits, preferred_element_type=jnp.float32
    ).astype(jnp.bfloat16)


def fit(wide, fitted_ref, orbitals, f_ref, at):
    slabs = jnp.concatenate([fitted_ref[o] for o in orbitals], axis=1)
    f_ref[at] = jnp.dot(wide, slabs, preferred_element_type=jnp.float32).astype(jnp.bfloat16)


def batches(count):
    return [range(first, min(first + GROUP, count)) for first in range(0, count, GROUP)]


def exch_kernel(count, per, npno, *refs):
    blocks, fitted_ref = refs[:count], refs[count]
    outs, amps_ref, (held_ref, occ_ref, wide_ref, f_ref, sem) = refs[-8:-6], refs[-6], refs[-5:]
    npao, width = fitted_ref.shape[1:]
    orbitals = read_orbitals(blocks, per, npno, held_ref, occ_ref, sem)
    orbitals.start()
    for k in range(count):
        amps_ref[k] = blocks[k][per * npno : (per + 1) * npno, :]
    codes = code(lax.broadcasted_iota(jnp.int32, (1, npao), 1))
    for group in batches(count * per):
        for at, pair in enumerate(group):
            k, p = divmod(pair, per)
            expand(blocks[k], p, codes, wide_ref, at)
        if group[0] == 0:
            orbitals.wait()
        for at, pair in enumerate(group):
            k, p = divmod(pair, per)
            fit(wide_ref[at], fitted_ref, [occ_ref[k, 2 * p + t] for t in range(2)], f_ref, at)
        for at, pair in enumerate(group):
            k, p = divmod(pair, per)
            half, k = divmod(k, count // 2)
            outs[half][k, :, p * npno : (p + 1) * npno] = contract(f_ref[at], width)


def gate_kernel(*refs):
    pass


def sum_kernel(plan, *refs):
    outs = refs[len(refs) - len(plan) :]
    for out_ref, terms in zip(outs, plan):
        for k, (first, *others) in enumerate(terms):
            total = refs[first[0]][first[1]].astype(jnp.float32)
            for ref, at in others:
                total = total + refs[ref][at].astype(jnp.float32)
            out_ref[k] = total.astype(out_ref.dtype)


def coupled_kernel(orders, *refs):
    amps_in, refs = refs[: len(orders)], refs[len(orders) :]
    where_ref, weight_ref, inter_ref, occ_ref, count_ref, occ_energy_ref, energy_ref, amps_ref = refs[:8]
    kept_ref, factor_ref, live_ref, all_ref, half_ref = refs[-5:]
    per, ncpl, npno = inter_ref.shape[:3]
    for order, ref in zip(orders, amps_in):
        for k, m in enumerate(order):
            for p in range(per):
                all_ref[m * per + p] = ref[k, :, p * npno : (p + 1) * npno]
    for p in range(per):
        for c in range(ncpl):
            half_ref[p * ncpl + c] = weight_ref[p, c] * jnp.dot(
                inter_ref[p, c], all_ref[where_ref[p, c]], preferred_element_type=jnp.float32
            )
    row = lax.broadcasted_iota(jnp.int32, (npno, npno), 0)
    col = lax.broadcasted_iota(jnp.int32, (npno, npno), 1)
    for p in range(per):
        total = jnp.zeros((npno, npno), jnp.float32)
        for c in range(ncpl):
            half = half_ref[p * ncpl + c]
            high = half.astype(jnp.bfloat16)
            low = (half - high.astype(jnp.float32)).astype(jnp.bfloat16)
            inter = inter_ref[p, c]
            total = total + lax.dot_general(high, inter, NT, preferred_element_type=jnp.float32)
            total = total + lax.dot_general(low, inter, NT, preferred_element_type=jnp.float32)
        here = slice(p * npno, (p + 1) * npno)
        across = jnp.broadcast_to(energy_ref[p : p + 1, :], (npno, npno))
        occ_pair = occ_energy_ref[occ_ref[0, p]] + occ_energy_ref[occ_ref[1, p]]
        denom = across.T + across - occ_pair
        live = jnp.where((row < count_ref[p]) & (col < count_ref[p]), jnp.float32(1), jnp.float32(0))
        factor = live / (denom + 0.5)
        amps = amps_ref[p]
        kept_ref[:, here] = live * amps - factor * (denom * amps + total)
        factor_ref[:, here] = factor
        live_ref[:, here] = live


def finish_kernel(own_ref, came_ref, late_ref, kept_ref, factor_ref, live_ref, new_ref, ints_ref):
    per, npno = new_ref.shape[:2]
    exch = own_ref[0] + came_ref[0].astype(jnp.float32) + late_ref[0].astype(jnp.float32)
    new = kept_ref[...] - exch * factor_ref[...]
    ints = exch * live_ref[...]
    for p in range(per):
        new_ref[p] = new[:, p * npno : (p + 1) * npno]
        ints_ref[p] = ints[:, p * npno : (p + 1) * npno]


def shards(
    fitted_ints,
    pno_basis,
    pair_occ,
    pair_dom,
    pno_count,
    pno_energy,
    occ_energy,
    amps,
    cpl_pair,
    cpl_weight,
    intersections,
):
    ndev = lax.axis_size("pairs")
    per, dom, npno = pno_basis.shape
    ncpl = cpl_pair.shape[1]
    npao, width = fitted_ints.shape[1:]
    params = pltpu.CompilerParams(vmem_limit_bytes=LIMIT)
    me = lax.axis_index("pairs")
    steps = [1 << b for b in reversed(range(1, ndev.bit_length() - 1))]

    def swap(array, mask):
        return lax.ppermute(array, "pairs", [(d, d ^ mask) for d in range(ndev)])

    first_block, block = pl.pallas_call(
        pack_kernel,
        out_shape=[jax.ShapeDtypeStruct(((per + 1) * npno + ROWS, dom), jnp.bfloat16)] * 2,
        in_specs=[HBM] * 4,
        out_specs=[VMEM] * 2,
        scratch_shapes=[
            pltpu.VMEM((per, dom), jnp.int32),
            pltpu.SMEM((2, per), jnp.int32),
            pltpu.VMEM((per, npno, npno), jnp.float32),
            pltpu.SemaphoreType.DMA((3 + 2 * per,)),
        ],
        compiler_params=pltpu.CompilerParams(vmem_limit_bytes=62 << 20),
    )(jnp.swapaxes(pno_basis, 1, 2), pair_dom, pair_occ.T, amps)

    def estimate(flops):
        return pl.CostEstimate(flops=flops, bytes_accessed=1 << 20, transcendentals=0)

    def gate(array, after=(), flops=0, held=False):
        return pl.pallas_call(
            gate_kernel,
            out_shape=jax.ShapeDtypeStruct(array.shape, array.dtype),
            in_specs=[HBM] * (1 + len(after)) + [VMEM] * held,
            out_specs=HBM,
            input_output_aliases={0: 0},
            compiler_params=params,
            cost_estimate=estimate(flops),
        )(array, *after, *[fitted_ints] * held)

    mine, chain, back, amps_of = {}, [], [], []

    def add_up(plan, dtypes, after=()):
        arrays = []
        for terms in plan:
            for term in terms:
                for array, _ in term:
                    if not any(array is a for a in arrays):
                        arrays.append(array)
        number = lambda array: [array is a for a in arrays].index(True)
        return pl.pallas_call(
            functools.partial(
                sum_kernel, [[[(number(array), at) for array, at in term] for term in terms] for terms in plan]
            ),
            out_shape=[
                jax.ShapeDtypeStruct((len(terms), npno, per * npno), dtype) for terms, dtype in zip(plan, dtypes)
            ],
            in_specs=[VMEM] * len(arrays) + [HBM] * len(after),
            out_specs=[VMEM] * len(plan),
            compiler_params=params,
        )(*arrays, *after)

    def exchange(which, cost=COST):
        count = 2 * len(which)
        after = chain[-1:] + (back[:-1][-1:] if far[-1] not in which else [])
        out = pl.pallas_call(
            functools.partial(exch_kernel, count, per, npno),
            out_shape=[jax.ShapeDtypeStruct((len(which), npno, per * npno), jnp.float32)] * 2
            + [jax.ShapeDtypeStruct((count, npno, dom), jnp.bfloat16)],
            in_specs=[VMEM] * (count + 1) + [HBM] * len(after),
            out_specs=[VMEM] * 3,
            scratch_shapes=[
                pltpu.VMEM((8, 128), jnp.int32),
                pltpu.SMEM((8, 128), jnp.int32),
                pltpu.VMEM((GROUP, npno, npao), jnp.bfloat16),
                pltpu.VMEM((GROUP, npno, 2 * width), jnp.bfloat16),
                pltpu.SemaphoreType.DMA,
            ],
            compiler_params=params,
            cost_estimate=estimate(cost * count * per),
        )(*[blocks[m] for m in which], *[blocks[m ^ 1] for m in which], fitted_ints, *after)
        chain.append(out[0])
        amps_of.append((out[2], list(which) + [m ^ 1 for m in which]))
        got = swap(out[1], 1)
        kinds = [[(k, m) for k, m in enumerate(which) if bool(m & steps[-1]) == far] for far in (False, True)]
        types = [dtype for kind, dtype in zip(kinds, (jnp.float32, SENT)) if kind]
        kinds = [kind for kind in kinds if kind]
        sums = add_up([[[(out[0], k), (got, k)] for k, _ in kind] for kind in kinds], types)
        for array, kind in zip(sums, kinds):
            for at, (_, m) in enumerate(kind):
                mine[m] = (array, at)
        back.append(sums[0])

    top, rest, last = steps[0], steps[1:], steps[-1]
    own = [0]
    for mask in steps[:-1]:
        own += [m ^ mask for m in own]
    far = [m ^ last for m in own]
    blocks = {top: swap(first_block, top)}
    block = blocks[0] = gate(block, (), 32 * COST)
    for mask in rest + [1]:
        blocks[mask] = swap(block, mask)
    exchange([0], 0)
    for m in rest:
        blocks[m ^ 1] = swap(blocks[m], 1)
    for m in rest[:-1]:
        blocks[m ^ last] = swap(blocks[m], last)
        blocks[m ^ last ^ 1] = swap(blocks[m ^ last], 1)
    blocks[top] = gate(blocks[top], chain[-1:], held=True)
    for mask in (rest[0], last):
        blocks[top ^ mask] = swap(blocks[top], mask)
    blocks[top ^ 1] = swap(blocks[top], 1)
    exchange(rest[::-1])
    blocks[top ^ rest[0]] = gate(blocks[top ^ rest[0]], chain[-1:], held=True)
    exchange([rest[0] ^ last, top])
    even = [0, top]
    for mask in rest:
        for m in list(even):
            if m ^ mask not in blocks:
                blocks[m ^ mask] = swap(blocks[m], mask)
            even.append(m ^ mask)
    left = [m for m in far[:-1] + own if m not in mine]
    for m in left:
        if m ^ 1 not in blocks:
            blocks[m ^ 1] = swap(blocks[m], 1)
    blocks[far[-1]] = gate(blocks[far[-1]], chain[-1:], held=True)
    blocks[far[-1] ^ 1] = swap(blocks[far[-1]], 1)
    for first in range(0, len(left), CALL):
        exchange(left[first : first + CALL])
    exchange(far[-1:])

    ready = add_up([[[mine[m]] for m in far[:-1]]], [SENT])[0]
    final = gate(mine[far[-1]][0], (), 32 * COST)
    late = final
    terms = [[mine[m]] for m in own]
    ready, final = swap(ready, last), swap(final, far[-1])
    for k in range(len(own) - 1):
        terms[k].append((ready, k))

    away = jnp.bitwise_xor(cpl_pair // per, me)
    where = away * per + cpl_pair % per
    kept, factor, live = pl.pallas_call(
        functools.partial(coupled_kernel, [order for _, order in amps_of]),
        out_shape=[jax.ShapeDtypeStruct((npno, per * npno), jnp.float32)] * 3,
        in_specs=[VMEM] * len(amps_of) + [SMEM, SMEM, VMEM, SMEM, SMEM, SMEM, VMEM, VMEM, HBM],
        out_specs=[VMEM] * 3,
        scratch_shapes=[
            pltpu.VMEM((ndev * per, npno, npno), jnp.bfloat16),
            pltpu.VMEM((per * ncpl, npno, npno), jnp.float32),
        ],
        compiler_params=params,
        cost_estimate=estimate(8 * COST),
    )(
        *[array for array, _ in amps_of],
        where,
        cpl_weight,
        intersections,
        pair_occ.T,
        pno_count,
        occ_energy,
        pno_energy,
        amps,
        late,
    )

    for mask in reversed(steps[:-1]):
        half = len(terms) // 2
        keep, send = add_up([terms[:half], terms[half:]], [jnp.float32, SENT], [kept] if mask == top else [])
        send = swap(send, mask)
        terms = [[(keep, k), (send, k)] for k in range(half)]

    return pl.pallas_call(
        finish_kernel,
        out_shape=[jax.ShapeDtypeStruct((per, npno, npno), jnp.float32)] * 2,
        in_specs=[VMEM] * 6,
        out_specs=[VMEM] * 2,
        compiler_params=params,
    )(keep, send, final, kept, factor, live)


def solution(mesh):
    both = ("groups", "pairs")
    in_specs = (
        P(None, None, both),
        P(both, None, None),
        P(both, None),
        P(both, None),
        P(both),
        P(both, None),
        P("groups"),
        P(both, None, None),
        P(both, None),
        P(both, None),
        P(both, None, None, None),
    )
    out_specs = (P(both, None, None), P(both, None, None))

    def run(*args):
        return tuple(jax.shard_map(shards, mesh=mesh, in_specs=in_specs, out_specs=out_specs, check_vma=False)(*args))

    return run
```

```python
import functools

import jax
import jax.numpy as jnp
from jax import lax
from jax.experimental import pallas as pl
from jax.experimental.pallas import tpu as pltpu
from jax.sharding import PartitionSpec as P

NT = (((1,), (1,)), ((), ()))
VMEM = pl.BlockSpec(memory_space=pltpu.VMEM)
HBM = pl.BlockSpec(memory_space=pltpu.HBM)
SMEM = pl.BlockSpec(memory_space=pltpu.SMEM)
SENT = jnp.bfloat16
LIMIT = 16 << 20
ROWS = 16
CALL = 2
COST = 300_000_000
GROUP = 16


def code(index):
    low = 128 + jnp.bitwise_and(index, 127)
    return lax.shift_left(low, lax.shift_right_logical(index, 7)).astype(jnp.float32).astype(jnp.bfloat16)


def pack_kernel(basis_ref, dom_ref, occ_ref, amps_ref, out_ref, again_ref, dom_in, occ_in, amps_in, sems):
    per, npno, dom = basis_ref.shape
    base = per * npno
    copies = [
        pltpu.make_async_copy(amps_ref, amps_in, sems.at[0]),
        pltpu.make_async_copy(dom_ref, dom_in, sems.at[1]),
        pltpu.make_async_copy(occ_ref, occ_in, sems.at[2]),
    ]
    for p in range(per):
        for k, ref in enumerate((out_ref, again_ref)):
            rows = ref.at[pl.ds(p * npno, npno)]
            copies.append(pltpu.make_async_copy(basis_ref.at[p], rows, sems.at[3 + 2 * p + k]))
    for copy in copies:
        copy.start()
    for copy in copies:
        copy.wait()
    lane = lax.broadcasted_iota(jnp.int32, (1, dom), 1)
    orbitals = jnp.zeros((1, dom), jnp.int32)
    for p in range(per):
        for t in range(2):
            orbitals = jnp.where(lane == 2 * p + t, occ_in[t, p], orbitals)
    tail = jnp.concatenate(
        [
            code(dom_in[...]).astype(jnp.float32),
            orbitals.astype(jnp.float32),
            jnp.zeros((ROWS - per - 1, dom), jnp.float32),
        ],
        axis=0,
    )
    for ref in (out_ref, again_ref):
        ref[base : base + npno, :] = jnp.concatenate(
            [amps_in[p].astype(jnp.bfloat16) for p in range(per)], axis=1
        )
        ref[base + npno :, :] = tail.astype(jnp.bfloat16)


def read_orbitals(blocks, per, npno, held_ref, occ_ref, sem):
    base = (per + 1) * npno
    for k, block in enumerate(blocks):
        tail = block[base : base + ROWS, :].astype(jnp.float32)
        held_ref[k : k + 1, :] = tail[per : per + 1, :128].astype(jnp.int32)
    return pltpu.make_async_copy(held_ref, occ_ref, sem)


def contract(both, width):
    return lax.dot_general(both[:, :width], both[:, width:], NT, preferred_element_type=jnp.float32)


def expand(block, p, codes, out_ref, at):
    npno, dom = out_ref.shape[1], block.shape[1]
    base = block.shape[0] - ROWS + p
    column = jnp.broadcast_to(block[base : base + 1, :], (128, dom)).T
    zero, one = jnp.bfloat16(0), jnp.bfloat16(1)
    hits = jnp.concatenate(
        [jnp.where(column == codes[:, q : q + 128], one, zero) for q in range(0, codes.shape[1], 128)], axis=1
    )
    out_ref[at] = jnp.dot(
        block[p * npno : (p + 1) * npno, :], hits, preferred_element_type=jnp.float32
    ).astype(jnp.bfloat16)


def fit(wide, fitted_ref, orbitals, f_ref, at):
    slabs = jnp.concatenate([fitted_ref[o] for o in orbitals], axis=1)
    f_ref[at] = jnp.dot(wide, slabs, preferred_element_type=jnp.float32).astype(jnp.bfloat16)


def batches(count):
    return [range(first, min(first + GROUP, count)) for first in range(0, count, GROUP)]


def exch_kernel(count, per, npno, *refs):
    blocks, fitted_ref = refs[:count], refs[count]
    outs, amps_ref, (held_ref, occ_ref, wide_ref, f_ref, sem) = refs[-8:-6], refs[-6], refs[-5:]
    npao, width = fitted_ref.shape[1:]
    orbitals = read_orbitals(blocks, per, npno, held_ref, occ_ref, sem)
    orbitals.start()
    for k in range(count):
        amps_ref[k] = blocks[k][per * npno : (per + 1) * npno, :]
    codes = code(lax.broadcasted_iota(jnp.int32, (1, npao), 1))
    for group in batches(count * per):
        for at, pair in enumerate(group):
            k, p = divmod(pair, per)
            expand(blocks[k], p, codes, wide_ref, at)
        if group[0] == 0:
            orbitals.wait()
        for at, pair in enumerate(group):
            k, p = divmod(pair, per)
            fit(wide_ref[at], fitted_ref, [occ_ref[k, 2 * p + t] for t in range(2)], f_ref, at)
        for at, pair in enumerate(group):
            k, p = divmod(pair, per)
            half, k = divmod(k, count // 2)
            outs[half][k, :, p * npno : (p + 1) * npno] = contract(f_ref[at], width)


def gate_kernel(*refs):
    pass


def sum_kernel(plan, *refs):
    outs = refs[len(refs) - len(plan) :]
    for out_ref, terms in zip(outs, plan):
        for k, (first, *others) in enumerate(terms):
            total = refs[first[0]][first[1]].astype(jnp.float32)
            for ref, at in others:
                total = total + refs[ref][at].astype(jnp.float32)
            out_ref[k] = total.astype(out_ref.dtype)


def coupled_kernel(orders, *refs):
    amps_in, refs = refs[: len(orders)], refs[len(orders) :]
    where_ref, weight_ref, inter_ref, occ_ref, count_ref, occ_energy_ref, energy_ref, amps_ref = refs[:8]
    kept_ref, factor_ref, live_ref, all_ref, half_ref = refs[-5:]
    per, ncpl, npno = inter_ref.shape[:3]
    for order, ref in zip(orders, amps_in):
        for k, m in enumerate(order):
            for p in range(per):
                all_ref[m * per + p] = ref[k, :, p * npno : (p + 1) * npno]
    for p in range(per):
        for c in range(ncpl):
            half_ref[p * ncpl + c] = weight_ref[p, c] * jnp.dot(
                inter_ref[p, c], all_ref[where_ref[p, c]], preferred_element_type=jnp.float32
            )
    row = lax.broadcasted_iota(jnp.int32, (npno, npno), 0)
    col = lax.broadcasted_iota(jnp.int32, (npno, npno), 1)
    for p in range(per):
        total = jnp.zeros((npno, npno), jnp.float32)
        for c in range(ncpl):
            half = half_ref[p * ncpl + c]
            high = half.astype(jnp.bfloat16)
            low = (half - high.astype(jnp.float32)).astype(jnp.bfloat16)
            inter = inter_ref[p, c]
            total = total + lax.dot_general(high, inter, NT, preferred_element_type=jnp.float32)
            total = total + lax.dot_general(low, inter, NT, preferred_element_type=jnp.float32)
        here = slice(p * npno, (p + 1) * npno)
        across = jnp.broadcast_to(energy_ref[p : p + 1, :], (npno, npno))
        occ_pair = occ_energy_ref[occ_ref[0, p]] + occ_energy_ref[occ_ref[1, p]]
        denom = across.T + across - occ_pair
        live = jnp.where((row < count_ref[p]) & (col < count_ref[p]), jnp.float32(1), jnp.float32(0))
        factor = live / (denom + 0.5)
        amps = amps_ref[p]
        kept_ref[:, here] = live * amps - factor * (denom * amps + total)
        factor_ref[:, here] = factor
        live_ref[:, here] = live


def finish_kernel(own_ref, came_ref, late_ref, kept_ref, factor_ref, live_ref, new_ref, ints_ref):
    per, npno = new_ref.shape[:2]
    exch = own_ref[0] + came_ref[0].astype(jnp.float32) + late_ref[0].astype(jnp.float32)
    new = kept_ref[...] - exch * factor_ref[...]
    ints = exch * live_ref[...]
    for p in range(per):
        new_ref[p] = new[:, p * npno : (p + 1) * npno]
        ints_ref[p] = ints[:, p * npno : (p + 1) * npno]


def shards(
    fitted_ints,
    pno_basis,
    pair_occ,
    pair_dom,
    pno_count,
    pno_energy,
    occ_energy,
    amps,
    cpl_pair,
    cpl_weight,
    intersections,
):
    ndev = lax.axis_size("pairs")
    per, dom, npno = pno_basis.shape
    ncpl = cpl_pair.shape[1]
    npao, width = fitted_ints.shape[1:]
    params = pltpu.CompilerParams(vmem_limit_bytes=LIMIT)
    me = lax.axis_index("pairs")
    steps = [1 << b for b in reversed(range(1, ndev.bit_length() - 1))]

    def swap(array, mask):
        return lax.ppermute(array, "pairs", [(d, d ^ mask) for d in range(ndev)])

    first_block, block = pl.pallas_call(
        pack_kernel,
        out_shape=[jax.ShapeDtypeStruct(((per + 1) * npno + ROWS, dom), jnp.bfloat16)] * 2,
        in_specs=[HBM] * 4,
        out_specs=[VMEM] * 2,
        scratch_shapes=[
            pltpu.VMEM((per, dom), jnp.int32),
            pltpu.SMEM((2, per), jnp.int32),
            pltpu.VMEM((per, npno, npno), jnp.float32),
            pltpu.SemaphoreType.DMA((3 + 2 * per,)),
        ],
        compiler_params=pltpu.CompilerParams(vmem_limit_bytes=62 << 20),
    )(jnp.swapaxes(pno_basis, 1, 2), pair_dom, pair_occ.T, amps)

    def estimate(flops):
        return pl.CostEstimate(flops=flops, bytes_accessed=1 << 20, transcendentals=0)

    def gate(array, after=(), flops=0, held=False):
        return pl.pallas_call(
            gate_kernel,
            out_shape=jax.ShapeDtypeStruct(array.shape, array.dtype),
            in_specs=[HBM] * (1 + len(after)) + [VMEM] * held,
            out_specs=HBM,
            input_output_aliases={0: 0},
            compiler_params=params,
            cost_estimate=estimate(flops),
        )(array, *after, *[fitted_ints] * held)

    mine, chain, back, amps_of = {}, [], [], []

    def add_up(plan, dtypes, after=()):
        arrays = []
        for terms in plan:
            for term in terms:
                for array, _ in term:
                    if not any(array is a for a in arrays):
                        arrays.append(array)
        number = lambda array: [array is a for a in arrays].index(True)
        return pl.pallas_call(
            functools.partial(
                sum_kernel, [[[(number(array), at) for array, at in term] for term in terms] for terms in plan]
            ),
            out_shape=[
                jax.ShapeDtypeStruct((len(terms), npno, per * npno), dtype) for terms, dtype in zip(plan, dtypes)
            ],
            in_specs=[VMEM] * len(arrays) + [HBM] * len(after),
            out_specs=[VMEM] * len(plan),
            compiler_params=params,
        )(*arrays, *after)

    def exchange(which, cost=COST):
        count = 2 * len(which)
        after = chain[-1:] + (back[:-1][-1:] if far[-1] not in which else [])
        out = pl.pallas_call(
            functools.partial(exch_kernel, count, per, npno),
            out_shape=[jax.ShapeDtypeStruct((len(which), npno, per * npno), jnp.float32)] * 2
            + [jax.ShapeDtypeStruct((count, npno, dom), jnp.bfloat16)],
            in_specs=[VMEM] * (count + 1) + [HBM] * len(after),
            out_specs=[VMEM] * 3,
            scratch_shapes=[
                pltpu.VMEM((8, 128), jnp.int32),
                pltpu.SMEM((8, 128), jnp.int32),
                pltpu.VMEM((GROUP, npno, npao), jnp.bfloat16),
                pltpu.VMEM((GROUP, npno, 2 * width), jnp.bfloat16),
                pltpu.SemaphoreType.DMA,
            ],
            compiler_params=params,
            cost_estimate=estimate(cost * count * per),
        )(*[blocks[m] for m in which], *[blocks[m ^ 1] for m in which], fitted_ints, *after)
        chain.append(out[0])
        amps_of.append((out[2], list(which) + [m ^ 1 for m in which]))
        got = swap(out[1], 1)
        kinds = [[(k, m) for k, m in enumerate(which) if bool(m & steps[-1]) == far] for far in (False, True)]
        types = [dtype for kind, dtype in zip(kinds, (jnp.float32, SENT)) if kind]
        kinds = [kind for kind in kinds if kind]
        sums = add_up([[[(out[0], k), (got, k)] for k, _ in kind] for kind in kinds], types)
        for array, kind in zip(sums, kinds):
            for at, (_, m) in enumerate(kind):
                mine[m] = (array, at)
        back.append(sums[0])

    top, rest, last = steps[0], steps[1:], steps[-1]
    own = [0]
    for mask in steps[:-1]:
        own += [m ^ mask for m in own]
    far = [m ^ last for m in own]
    blocks = {top: swap(first_block, top)}
    block = blocks[0] = gate(block, (), 32 * COST)
    for mask in rest + [1]:
        blocks[mask] = swap(block, mask)
    exchange([0], 0)
    for m in rest:
        blocks[m ^ 1] = swap(blocks[m], 1)
    for m in rest[:-1]:
        blocks[m ^ last] = swap(blocks[m], last)
        blocks[m ^ last ^ 1] = swap(blocks[m ^ last], 1)
    blocks[top] = gate(blocks[top], chain[-1:], held=True)
    for mask in (rest[0], last):
        blocks[top ^ mask] = swap(blocks[top], mask)
    blocks[top ^ 1] = swap(blocks[top], 1)
    exchange(rest[::-1])
    blocks[top ^ rest[0]] = gate(blocks[top ^ rest[0]], chain[-1:], held=True)
    exchange([rest[0] ^ last, top])
    even = [0, top]
    for mask in rest:
        for m in list(even):
            if m ^ mask not in blocks:
                blocks[m ^ mask] = swap(blocks[m], mask)
            even.append(m ^ mask)
    left = [m for m in far[:-1] + own if m not in mine]
    for m in left:
        if m ^ 1 not in blocks:
            blocks[m ^ 1] = swap(blocks[m], 1)
    blocks[far[-1]] = gate(blocks[far[-1]], chain[-1:], held=True)
    blocks[far[-1] ^ 1] = swap(blocks[far[-1]], 1)
    for first in range(0, len(left), CALL):
        exchange(left[first : first + CALL])
    exchange(far[-1:])

    ready = add_up([[[mine[m]] for m in far[:-1]]], [SENT])[0]
    final = gate(mine[far[-1]][0], (), 32 * COST)
    terms = [[mine[m]] for m in own]
    ready, final = swap(ready, last), swap(final, far[-1])
    for k in range(len(own) - 1):
        terms[k].append((ready, k))

    for mask in reversed(steps[:-1]):
        half = len(terms) // 2
        keep, send = add_up([terms[:half], terms[half:]], [jnp.float32, SENT])
        send = swap(send, mask)
        terms = [[(keep, k), (send, k)] for k in range(half)]

    away = jnp.bitwise_xor(cpl_pair // per, me)
    where = away * per + cpl_pair % per
    kept, factor, live = pl.pallas_call(
        functools.partial(coupled_kernel, [order for _, order in amps_of]),
        out_shape=[jax.ShapeDtypeStruct((npno, per * npno), jnp.float32)] * 3,
        in_specs=[VMEM] * len(amps_of) + [SMEM, SMEM, VMEM, SMEM, SMEM, SMEM, VMEM, VMEM, HBM],
        out_specs=[VMEM] * 3,
        scratch_shapes=[
            pltpu.VMEM((ndev * per, npno, npno), jnp.bfloat16),
            pltpu.VMEM((per * ncpl, npno, npno), jnp.float32),
        ],
        compiler_params=params,
        cost_estimate=estimate(8 * COST),
    )(
        *[array for array, _ in amps_of],
        where,
        cpl_weight,
        intersections,
        pair_occ.T,
        pno_count,
        occ_energy,
        pno_energy,
        amps,
        keep,
    )

    return pl.pallas_call(
        finish_kernel,
        out_shape=[jax.ShapeDtypeStruct((per, npno, npno), jnp.float32)] * 2,
        in_specs=[VMEM] * 6,
        out_specs=[VMEM] * 2,
        compiler_params=params,
    )(keep, send, final, kept, factor, live)


def solution(mesh):
    both = ("groups", "pairs")
    in_specs = (
        P(None, None, both),
        P(both, None, None),
        P(both, None),
        P(both, None),
        P(both),
        P(both, None),
        P("groups"),
        P(both, None, None),
        P(both, None),
        P(both, None),
        P(both, None, None, None),
    )
    out_specs = (P(both, None, None), P(both, None, None))

    def run(*args):
        return tuple(jax.shard_map(shards, mesh=mesh, in_specs=in_specs, out_specs=out_specs, check_vma=False)(*args))

    return run
```

```python
import functools

import jax
import jax.numpy as jnp
from jax import lax
from jax.experimental import pallas as pl
from jax.experimental.pallas import tpu as pltpu
from jax.sharding import PartitionSpec as P

NT = (((1,), (1,)), ((), ()))
VMEM = pl.BlockSpec(memory_space=pltpu.VMEM)
HBM = pl.BlockSpec(memory_space=pltpu.HBM)
SMEM = pl.BlockSpec(memory_space=pltpu.SMEM)
SENT = jnp.bfloat16
LIMIT = 16 << 20
ROWS = 16
CALL = 2
COST = 300_000_000
GROUP = 16


def code(index):
    low = 128 + jnp.bitwise_and(index, 127)
    return lax.shift_left(low, lax.shift_right_logical(index, 7)).astype(jnp.float32).astype(jnp.bfloat16)


def pack_kernel(basis_ref, dom_ref, occ_ref, amps_ref, out_ref, again_ref, dom_in, occ_in, amps_in, sems):
    per, npno, dom = basis_ref.shape
    base = per * npno
    copies = [
        pltpu.make_async_copy(amps_ref, amps_in, sems.at[0]),
        pltpu.make_async_copy(dom_ref, dom_in, sems.at[1]),
        pltpu.make_async_copy(occ_ref, occ_in, sems.at[2]),
    ]
    for p in range(per):
        for k, ref in enumerate((out_ref, again_ref)):
            rows = ref.at[pl.ds(p * npno, npno)]
            copies.append(pltpu.make_async_copy(basis_ref.at[p], rows, sems.at[3 + 2 * p + k]))
    for copy in copies:
        copy.start()
    for copy in copies:
        copy.wait()
    lane = lax.broadcasted_iota(jnp.int32, (1, dom), 1)
    orbitals = jnp.zeros((1, dom), jnp.int32)
    for p in range(per):
        for t in range(2):
            orbitals = jnp.where(lane == 2 * p + t, occ_in[t, p], orbitals)
    tail = jnp.concatenate(
        [
            code(dom_in[...]).astype(jnp.float32),
            orbitals.astype(jnp.float32),
            jnp.zeros((ROWS - per - 1, dom), jnp.float32),
        ],
        axis=0,
    )
    for ref in (out_ref, again_ref):
        ref[base : base + npno, :] = jnp.concatenate(
            [amps_in[p].astype(jnp.bfloat16) for p in range(per)], axis=1
        )
        ref[base + npno :, :] = tail.astype(jnp.bfloat16)


def read_orbitals(blocks, per, npno, held_ref, occ_ref, sem):
    base = (per + 1) * npno
    for k, block in enumerate(blocks):
        tail = block[base : base + ROWS, :].astype(jnp.float32)
        held_ref[k : k + 1, :] = tail[per : per + 1, :128].astype(jnp.int32)
    return pltpu.make_async_copy(held_ref, occ_ref, sem)


def contract(both, width):
    return lax.dot_general(both[:, :width], both[:, width:], NT, preferred_element_type=jnp.float32)


def expand(block, p, codes, out_ref, at):
    npno, dom = out_ref.shape[1], block.shape[1]
    base = block.shape[0] - ROWS + p
    column = jnp.broadcast_to(block[base : base + 1, :], (128, dom)).T
    zero, one = jnp.bfloat16(0), jnp.bfloat16(1)
    hits = jnp.concatenate(
        [jnp.where(column == codes[:, q : q + 128], one, zero) for q in range(0, codes.shape[1], 128)], axis=1
    )
    out_ref[at] = jnp.dot(
        block[p * npno : (p + 1) * npno, :], hits, preferred_element_type=jnp.float32
    ).astype(jnp.bfloat16)


def fit(wide, fitted_ref, orbitals, f_ref, at):
    slabs = jnp.concatenate([fitted_ref[o] for o in orbitals], axis=1)
    f_ref[at] = jnp.dot(wide, slabs, preferred_element_type=jnp.float32).astype(jnp.bfloat16)


def batches(count):
    return [range(first, min(first + GROUP, count)) for first in range(0, count, GROUP)]


def exch_kernel(count, per, npno, *refs):
    blocks, fitted_ref = refs[:count], refs[count]
    outs, amps_ref, (held_ref, occ_ref, wide_ref, f_ref, sem) = refs[-8:-6], refs[-6], refs[-5:]
    npao, width = fitted_ref.shape[1:]
    orbitals = read_orbitals(blocks, per, npno, held_ref, occ_ref, sem)
    orbitals.start()
    for k in range(count):
        amps_ref[k] = blocks[k][per * npno : (per + 1) * npno, :]
    codes = code(lax.broadcasted_iota(jnp.int32, (1, npao), 1))
    for group in batches(count * per):
        for at, pair in enumerate(group):
            k, p = divmod(pair, per)
            expand(blocks[k], p, codes, wide_ref, at)
        if group[0] == 0:
            orbitals.wait()
        for at, pair in enumerate(group):
            k, p = divmod(pair, per)
            fit(wide_ref[at], fitted_ref, [occ_ref[k, 2 * p + t] for t in range(2)], f_ref, at)
        for at, pair in enumerate(group):
            k, p = divmod(pair, per)
            half, k = divmod(k, count // 2)
            outs[half][k, :, p * npno : (p + 1) * npno] = contract(f_ref[at], width)


def gate_kernel(*refs):
    pass


def sum_kernel(plan, *refs):
    outs = refs[len(refs) - len(plan) :]
    for out_ref, terms in zip(outs, plan):
        for k, (first, *others) in enumerate(terms):
            total = refs[first[0]][first[1]].astype(jnp.float32)
            for ref, at in others:
                total = total + refs[ref][at].astype(jnp.float32)
            out_ref[k] = total.astype(out_ref.dtype)


def coupled_kernel(orders, *refs):
    amps_in, refs = refs[: len(orders)], refs[len(orders) :]
    where_ref, weight_ref, inter_ref, occ_ref, count_ref, occ_energy_ref, energy_ref, amps_ref = refs[:8]
    kept_ref, factor_ref, live_ref, all_ref, half_ref = refs[-5:]
    per, ncpl, npno = inter_ref.shape[:3]
    for order, ref in zip(orders, amps_in):
        for k, m in enumerate(order):
            for p in range(per):
                all_ref[m * per + p] = ref[k, :, p * npno : (p + 1) * npno]
    for p in range(per):
        for c in range(ncpl):
            half_ref[p * ncpl + c] = weight_ref[p, c] * jnp.dot(
                inter_ref[p, c], all_ref[where_ref[p, c]], preferred_element_type=jnp.float32
            )
    row = lax.broadcasted_iota(jnp.int32, (npno, npno), 0)
    col = lax.broadcasted_iota(jnp.int32, (npno, npno), 1)
    for p in range(per):
        total = jnp.zeros((npno, npno), jnp.float32)
        for first in range(0, ncpl, 4):
            some = range(first, min(first + 4, ncpl))
            half = jnp.concatenate([half_ref[p * ncpl + c] for c in some], axis=1)
            high = half.astype(jnp.bfloat16)
            low = (half - high.astype(jnp.float32)).astype(jnp.bfloat16)
            inter = jnp.concatenate([inter_ref[p, c] for c in some], axis=1)
            total = total + lax.dot_general(high, inter, NT, preferred_element_type=jnp.float32)
            total = total + lax.dot_general(low, inter, NT, preferred_element_type=jnp.float32)
        here = slice(p * npno, (p + 1) * npno)
        across = jnp.broadcast_to(energy_ref[p : p + 1, :], (npno, npno))
        occ_pair = occ_energy_ref[occ_ref[0, p]] + occ_energy_ref[occ_ref[1, p]]
        denom = across.T + across - occ_pair
        live = jnp.where((row < count_ref[p]) & (col < count_ref[p]), jnp.float32(1), jnp.float32(0))
        factor = live / (denom + 0.5)
        amps = amps_ref[p]
        kept_ref[:, here] = live * amps - factor * (denom * amps + total)
        factor_ref[:, here] = factor
        live_ref[:, here] = live


def finish_kernel(own_ref, came_ref, late_ref, kept_ref, factor_ref, live_ref, new_ref, ints_ref):
    per, npno = new_ref.shape[:2]
    exch = own_ref[0] + came_ref[0].astype(jnp.float32) + late_ref[0].astype(jnp.float32)
    new = kept_ref[...] - exch * factor_ref[...]
    ints = exch * live_ref[...]
    for p in range(per):
        new_ref[p] = new[:, p * npno : (p + 1) * npno]
        ints_ref[p] = ints[:, p * npno : (p + 1) * npno]


def shards(
    fitted_ints,
    pno_basis,
    pair_occ,
    pair_dom,
    pno_count,
    pno_energy,
    occ_energy,
    amps,
    cpl_pair,
    cpl_weight,
    intersections,
):
    ndev = lax.axis_size("pairs")
    per, dom, npno = pno_basis.shape
    ncpl = cpl_pair.shape[1]
    npao, width = fitted_ints.shape[1:]
    params = pltpu.CompilerParams(vmem_limit_bytes=LIMIT)
    me = lax.axis_index("pairs")
    steps = [1 << b for b in reversed(range(1, ndev.bit_length() - 1))]

    def swap(array, mask):
        return lax.ppermute(array, "pairs", [(d, d ^ mask) for d in range(ndev)])

    first_block, block = pl.pallas_call(
        pack_kernel,
        out_shape=[jax.ShapeDtypeStruct(((per + 1) * npno + ROWS, dom), jnp.bfloat16)] * 2,
        in_specs=[HBM] * 4,
        out_specs=[VMEM] * 2,
        scratch_shapes=[
            pltpu.VMEM((per, dom), jnp.int32),
            pltpu.SMEM((2, per), jnp.int32),
            pltpu.VMEM((per, npno, npno), jnp.float32),
            pltpu.SemaphoreType.DMA((3 + 2 * per,)),
        ],
        compiler_params=pltpu.CompilerParams(vmem_limit_bytes=62 << 20),
    )(jnp.swapaxes(pno_basis, 1, 2), pair_dom, pair_occ.T, amps)

    def estimate(flops):
        return pl.CostEstimate(flops=flops, bytes_accessed=1 << 20, transcendentals=0)

    def gate(array, after=(), flops=0, held=False):
        return pl.pallas_call(
            gate_kernel,
            out_shape=jax.ShapeDtypeStruct(array.shape, array.dtype),
            in_specs=[HBM] * (1 + len(after)) + [VMEM] * held,
            out_specs=HBM,
            input_output_aliases={0: 0},
            compiler_params=params,
            cost_estimate=estimate(flops),
        )(array, *after, *[fitted_ints] * held)

    mine, chain, back, amps_of = {}, [], [], []

    def add_up(plan, dtypes, after=()):
        arrays = []
        for terms in plan:
            for term in terms:
                for array, _ in term:
                    if not any(array is a for a in arrays):
                        arrays.append(array)
        number = lambda array: [array is a for a in arrays].index(True)
        return pl.pallas_call(
            functools.partial(
                sum_kernel, [[[(number(array), at) for array, at in term] for term in terms] for terms in plan]
            ),
            out_shape=[
                jax.ShapeDtypeStruct((len(terms), npno, per * npno), dtype) for terms, dtype in zip(plan, dtypes)
            ],
            in_specs=[VMEM] * len(arrays) + [HBM] * len(after),
            out_specs=[VMEM] * len(plan),
            compiler_params=params,
        )(*arrays, *after)

    def exchange(which, cost=COST):
        count = 2 * len(which)
        after = chain[-1:] + (back[:-1][-1:] if far[-1] not in which else [])
        out = pl.pallas_call(
            functools.partial(exch_kernel, count, per, npno),
            out_shape=[jax.ShapeDtypeStruct((len(which), npno, per * npno), jnp.float32)] * 2
            + [jax.ShapeDtypeStruct((count, npno, dom), jnp.bfloat16)],
            in_specs=[VMEM] * (count + 1) + [HBM] * len(after),
            out_specs=[VMEM] * 3,
            scratch_shapes=[
                pltpu.VMEM((8, 128), jnp.int32),
                pltpu.SMEM((8, 128), jnp.int32),
                pltpu.VMEM((GROUP, npno, npao), jnp.bfloat16),
                pltpu.VMEM((GROUP, npno, 2 * width), jnp.bfloat16),
                pltpu.SemaphoreType.DMA,
            ],
            compiler_params=params,
            cost_estimate=estimate(cost * count * per),
        )(*[blocks[m] for m in which], *[blocks[m ^ 1] for m in which], fitted_ints, *after)
        chain.append(out[0])
        amps_of.append((out[2], list(which) + [m ^ 1 for m in which]))
        got = swap(out[1], 1)
        kinds = [[(k, m) for k, m in enumerate(which) if bool(m & steps[-1]) == far] for far in (False, True)]
        types = [dtype for kind, dtype in zip(kinds, (jnp.float32, SENT)) if kind]
        kinds = [kind for kind in kinds if kind]
        sums = add_up([[[(out[0], k), (got, k)] for k, _ in kind] for kind in kinds], types)
        for array, kind in zip(sums, kinds):
            for at, (_, m) in enumerate(kind):
                mine[m] = (array, at)
        back.append(sums[0])

    top, rest, last = steps[0], steps[1:], steps[-1]
    own = [0]
    for mask in steps[:-1]:
        own += [m ^ mask for m in own]
    far = [m ^ last for m in own]
    blocks = {top: swap(first_block, top)}
    block = blocks[0] = gate(block, (), 32 * COST)
    for mask in rest + [1]:
        blocks[mask] = swap(block, mask)
    exchange([0], 0)
    for m in rest:
        blocks[m ^ 1] = swap(blocks[m], 1)
    for m in rest[:-1]:
        blocks[m ^ last] = swap(blocks[m], last)
        blocks[m ^ last ^ 1] = swap(blocks[m ^ last], 1)
    blocks[top] = gate(blocks[top], chain[-1:], held=True)
    for mask in (rest[0], last):
        blocks[top ^ mask] = swap(blocks[top], mask)
    blocks[top ^ 1] = swap(blocks[top], 1)
    exchange(rest[::-1])
    blocks[top ^ rest[0]] = gate(blocks[top ^ rest[0]], chain[-1:], held=True)
    exchange([rest[0] ^ last, top])
    even = [0, top]
    for mask in rest:
        for m in list(even):
            if m ^ mask not in blocks:
                blocks[m ^ mask] = swap(blocks[m], mask)
            even.append(m ^ mask)
    left = [m for m in far[:-1] + own if m not in mine]
    for m in left:
        if m ^ 1 not in blocks:
            blocks[m ^ 1] = swap(blocks[m], 1)
    blocks[far[-1]] = gate(blocks[far[-1]], chain[-1:], held=True)
    blocks[far[-1] ^ 1] = swap(blocks[far[-1]], 1)
    for first in range(0, len(left), CALL):
        exchange(left[first : first + CALL])
    exchange(far[-1:])

    ready = add_up([[[mine[m]] for m in far[:-1]]], [SENT])[0]
    final = gate(mine[far[-1]][0], (), 32 * COST)
    terms = [[mine[m]] for m in own]
    ready, final = swap(ready, last), swap(final, far[-1])
    for k in range(len(own) - 1):
        terms[k].append((ready, k))

    for mask in reversed(steps[:-1]):
        half = len(terms) // 2
        keep, send = add_up([terms[:half], terms[half:]], [jnp.float32, SENT])
        send = swap(send, mask)
        terms = [[(keep, k), (send, k)] for k in range(half)]

    away = jnp.bitwise_xor(cpl_pair // per, me)
    where = away * per + cpl_pair % per
    kept, factor, live = pl.pallas_call(
        functools.partial(coupled_kernel, [order for _, order in amps_of]),
        out_shape=[jax.ShapeDtypeStruct((npno, per * npno), jnp.float32)] * 3,
        in_specs=[VMEM] * len(amps_of) + [SMEM, SMEM, VMEM, SMEM, SMEM, SMEM, VMEM, VMEM, HBM],
        out_specs=[VMEM] * 3,
        scratch_shapes=[
            pltpu.VMEM((ndev * per, npno, npno), jnp.bfloat16),
            pltpu.VMEM((per * ncpl, npno, npno), jnp.float32),
        ],
        compiler_params=params,
        cost_estimate=estimate(8 * COST),
    )(
        *[array for array, _ in amps_of],
        where,
        cpl_weight,
        intersections,
        pair_occ.T,
        pno_count,
        occ_energy,
        pno_energy,
        amps,
        keep,
    )

    return pl.pallas_call(
        finish_kernel,
        out_shape=[jax.ShapeDtypeStruct((per, npno, npno), jnp.float32)] * 2,
        in_specs=[VMEM] * 6,
        out_specs=[VMEM] * 2,
        compiler_params=params,
    )(keep, send, final, kept, factor, live)


def solution(mesh):
    both = ("groups", "pairs")
    in_specs = (
        P(None, None, both),
        P(both, None, None),
        P(both, None),
        P(both, None),
        P(both),
        P(both, None),
        P("groups"),
        P(both, None, None),
        P(both, None),
        P(both, None),
        P(both, None, None, None),
    )
    out_specs = (P(both, None, None), P(both, None, None))

    def run(*args):
        return tuple(jax.shard_map(shards, mesh=mesh, in_specs=in_specs, out_specs=out_specs, check_vma=False)(*args))

    return run
```
